256 devices in a mesh: row: 32 (over z, y_lo, core), col: 2 (over y_hi), feat: 4 (over x).
Axes of the slice: x: 4, y: 4 (y_hi: 2, y_lo: 2; y = y_hi * 2 + y_lo), z: 8, core: 2. Of those that a mesh axis runs over, the one named last changes fastest.
Arguments:
- cotangent: bfloat16 [256, 65536], P('feat', ('row', 'col')), may hold values from -6 to 6
- preact: bfloat16 [256, 65536], P('feat', ('row', 'col')), may hold values from -6 to 6
- features: bfloat16 [256, 65536], P(None, ('row', 'col')), may hold values from -6 to 6
- aggregated: bfloat16 [256, 65536], P(None, ('row', 'col')), may hold values from -6 to 6
- w_self: bfloat16 [256, 256], replicated, may hold values from -0.375 to 0.375
- w_neigh: bfloat16 [256, 256], replicated, may hold values from -0.375 to 0.375
- tile_rows: int32 [16384], P(('row', 'col')), may hold values from 0 to 511, as said below
- tile_cols: int32 [16384], P(('row', 'col')), may hold values from 0 to 511, as said below
- tile_vals: bfloat16 [16384, 128, 128], P(('row', 'col')), may hold values from -0.09375 to 0.09375
- tile_live: int32 [64], P(('row', 'col')), may hold values from 1 to 256, as said below
Outputs:
- input_grad: bfloat16 [256, 65536], P('feat', ('row', 'col'))
- grad_self: float32 [256, 256], P(None, 'feat')
- grad_neigh: float32 [256, 256], P(None, 'feat')
The draws below stay inside these ranges and needn't reach their ends.
Inputs may be any that keep to these rules, and one draw needn't show every extreme that they name: `tile_rows`: slot s lies in group g = s // 256, g = r * 2 + c; its row block lies among the 2 * 8 blocks from r * 2 * 8 onward. Several slots may name the same block pair. `tile_cols`: with g = r * 2 + c as above, the column block of slot s is q * 2 * 8 + c * 8 + u for some q < 32 and u < 8. `tile_live`: some group has all 256 slots live in every draw.
All inputs are finite; a program needn't handle non-finite values.
Results may differ from the reference program's by a relative error of at most 0.0033.
Values may be sent and summed in bfloat16 or wider, within the bound.
No kernel may reach another device: no remote copies, remote signals or barrier semaphores. Data moves between devices by JAX's collectives and lax.ppermute only.
A program may use at most 128 MiB of HBM per device.

```python
import jax
import jax.numpy as jnp
from jax import lax

F_IN = 256
F_OUT = 256
NODE_DEV = 1024
TILES_DEV = 256
GRID_DEVS = 64
NODES = 65536
SLOTS = 16384
N_ROW = 32
N_COL = 2


def draw_tile_rows(key, part):
    key = jax.random.fold_in(key, 11)
    slot_ids = jnp.arange(SLOTS)
    owner = slot_ids // TILES_DEV
    row_pos = owner // N_COL
    row_span = N_COL * NODE_DEV // 128
    offset = jax.random.randint(key, (SLOTS,), 0, row_span)
    return (row_pos * row_span + offset).astype(jnp.int32)


def draw_tile_cols(key, part):
    key = jax.random.fold_in(key, 23)
    first_key, second_key = jax.random.split(key)
    slot_ids = jnp.arange(SLOTS)
    owner = slot_ids // TILES_DEV
    col_pos = owner % N_COL
    col_span = NODE_DEV // 128
    source_row = jax.random.randint(first_key, (SLOTS,), 0, N_ROW)
    within = jax.random.randint(second_key, (SLOTS,), 0, col_span)
    return (source_row * N_COL * col_span + col_pos * col_span + within).astype(jnp.int32)


def draw_tile_live(key, part):
    key = jax.random.fold_in(key, 37)
    first_key, second_key, third_key = jax.random.split(key, 3)
    first_factor = jax.random.randint(first_key, (GRID_DEVS,), 1, 5)
    second_factor = jax.random.randint(second_key, (GRID_DEVS,), 1, 5)
    live_count = jnp.maximum(TILES_DEV * first_factor * second_factor // 16, 1)
    chosen = jax.random.randint(third_key, (), 0, GRID_DEVS)
    live_count = jnp.where(jnp.arange(GRID_DEVS) == chosen, TILES_DEV, live_count)
    return live_count.astype(jnp.int32)


def block_levels(stream_key, extent, cuts, smallest, high):
    def one(position, blocks):
        steps = jax.random.uniform(jax.random.fold_in(jax.random.fold_in(stream_key, 6), position), (blocks,), jnp.float32, smallest / len(cuts), high / len(cuts))
        return jnp.repeat(jnp.exp(steps), extent[position] // blocks).reshape((-1,) + (1,) * (len(extent) - position - 1))

    level = one(*cuts[0])
    for cut in cuts[1:]:
        level = level * one(*cut)
    return level


def scatter_about(rng, shape, deviation, reach, shards=(), held_as=jnp.bfloat16):
    entries = deviation * jax.random.normal(rng, shape, jnp.float32)
    if shards:
        entries = entries * block_levels(rng, shape, shards, -0.22, 0.18)
    return jnp.clip(entries, -reach, reach).astype(held_as)


def setup_inputs(seed: int = 0) -> dict:
    key_of = jax.random.split(jax.random.key(seed), 11)
    cotangent = scatter_about(key_of[0], (F_OUT, NODES), 1.0, 6.0, ((0, 4), (1, 64)))
    preact = scatter_about(key_of[1], (F_OUT, NODES), 1.0, 6.0, ((0, 4), (1, 64)))
    features = scatter_about(key_of[2], (F_IN, NODES), 1.0, 6.0, ((1, 64),))
    aggregated = scatter_about(key_of[3], (F_IN, NODES), 1.0, 6.0, ((1, 64),))
    w_self = scatter_about(key_of[4], (F_IN, F_OUT), F_OUT ** -0.5, 0.375)
    w_neigh = scatter_about(key_of[5], (F_IN, F_OUT), F_OUT ** -0.5, 0.375)
    tile_rows = draw_tile_rows(jax.random.fold_in(key_of[10], 71), 0)
    tile_cols = draw_tile_cols(jax.random.fold_in(key_of[10], 71), 0)
    tile_vals = scatter_about(key_of[8], (SLOTS, 128, 128), (TILES_DEV * 16384 // NODE_DEV) ** -0.5, 0.09375, ((0, 64),))
    tile_live = draw_tile_live(jax.random.fold_in(key_of[10], 71), 0)
    return {"cotangent": cotangent, "preact": preact, "features": features, "aggregated": aggregated, "w_self": w_self, "w_neigh": w_neigh, "tile_rows": tile_rows, "tile_cols": tile_cols, "tile_vals": tile_vals, "tile_live": tile_live}


def reference(cotangent, preact, features, aggregated, w_self, w_neigh, tile_rows, tile_cols, tile_vals, tile_live):
    delta = jnp.where(preact > 0, cotangent, jnp.zeros_like(cotangent))
    grad_self = lax.dot_general(features, delta, (((1,), (1,)), ((), ())), preferred_element_type=jnp.float32)
    grad_neigh = lax.dot_general(aggregated, delta, (((1,), (1,)), ((), ())), preferred_element_type=jnp.float32)
    propagated = jnp.dot(w_neigh, delta, preferred_element_type=jnp.float32).astype(jnp.bfloat16)
    self_term = jnp.dot(w_self, delta, preferred_element_type=jnp.float32)
    blocks = propagated.reshape(F_IN, NODES // 128, 128).transpose(1, 0, 2)
    rows_all = tile_rows.reshape(GRID_DEVS, TILES_DEV)
    cols_all = tile_cols.reshape(GRID_DEVS, TILES_DEV)
    vals_all = tile_vals.reshape(GRID_DEVS, TILES_DEV, 128, 128)

    def one_group(totals, item):
        rows_now, cols_now, vals_now, live_count = item
        pieces = blocks[rows_now].astype(jnp.float32)
        products = jnp.einsum("sfi,sij->sfj", pieces, vals_now.astype(jnp.float32))
        keep_mask = (jnp.arange(TILES_DEV) < live_count).astype(jnp.float32)
        products = products * keep_mask[:, None, None]
        return totals.at[cols_now].add(products), None

    empty = jnp.zeros((NODES // 128, F_IN, 128), jnp.float32)
    totals, _ = lax.scan(one_group, empty, (rows_all, cols_all, vals_all, tile_live))
    summed = totals.transpose(1, 0, 2).reshape(F_IN, NODES)
    input_grad = (summed + self_term).astype(jnp.bfloat16)
    return (input_grad, grad_self, grad_neigh)
```

```python
import jax
import jax.numpy as jnp
from jax import lax
from jax.experimental import pallas as pl
from jax.experimental.pallas import tpu as pltpu
from jax.sharding import Mesh, PartitionSpec as P

AXES = ("z", "pair", "core", "half", "x")
BLOCK = 128
GROUP = 8
DEPTH = 4
ROOM = 256 + GROUP


def swap(n):
    return [(i, i ^ 1) for i in range(n)]


def turn(k, n):
    return [(i, (i + k) % n) for i in range(n)]


EVEN_PAIRS = swap(8)
ODD_PAIRS = [(i, (((i + 1) % 8 ^ 1) - 1) % 8) for i in range(8)]


def list_kernel(live_ref, entry_ref, mine_ref, lists_ref, count_ref):
    def place(slot, counts):
        other, own = counts
        mine = mine_ref[slot]
        lists_ref[jnp.where(mine == 1, ROOM + own, other)] = entry_ref[slot]
        return other + 1 - mine, own + mine

    other, own = lax.fori_loop(0, live_ref[0], place, (jnp.int32(0), jnp.int32(0)))
    for k in range(GROUP):
        lists_ref[other + k] = jnp.int32(BLOCK)
        lists_ref[ROOM + own + k] = jnp.int32(BLOCK)
    count_ref[0] = other
    count_ref[1] = own


def make_lists(live, entries, mine):
    smem = pl.BlockSpec(memory_space=pltpu.SMEM)
    return pl.pallas_call(
        list_kernel,
        out_shape=(jax.ShapeDtypeStruct((2 * ROOM,), jnp.int32), jax.ShapeDtypeStruct((2,), jnp.int32)),
        in_specs=[smem] * 3,
        out_specs=(smem, smem),
    )(live, entries, mine)


def tile_kernel(which, lists_ref, count_ref, near_ref, far_ref, vals_ref, out_ref, total, panel, tiles, sems):
    base = which * ROOM
    steps = (count_ref[which] + GROUP - 1) // GROUP

    def fetch(step):
        slot = lax.rem(step, DEPTH)
        for k in range(GROUP):
            entry = lists_ref[base + step * GROUP + k]
            pltpu.make_async_copy(
                vals_ref.at[lax.shift_right_logical(entry, 16)], tiles.at[slot * GROUP + k], sems.at[slot]
            ).start()

    for s in range(DEPTH - 1):
        pl.when(s < steps)(lambda s=s: fetch(jnp.int32(s)))
    panel[0:8] = near_ref[...]
    panel[8:16] = far_ref[...]
    total[...] = jnp.zeros_like(total)

    def body(step, carry):
        slot = lax.rem(step, DEPTH)
        pl.when(step + DEPTH - 1 < steps)(lambda: fetch(step + DEPTH - 1))
        held = tiles.at[pl.ds(slot * GROUP, GROUP)]
        pltpu.make_async_copy(vals_ref.at[pl.ds(0, GROUP)], held, sems.at[slot]).wait()
        places, products = [], []
        for k in range(GROUP):
            entry = lists_ref[base + step * GROUP + k]
            block = lax.shift_right_logical(entry, 8) & 255
            places.append(entry & 255)
            products.append(jnp.dot(panel[block], held[k], preferred_element_type=jnp.float32))
        for place, product in zip(places, products):
            total[place] += product
        return carry

    lax.fori_loop(0, steps, body, 0)
    out_ref[...] = total[0:BLOCK].astype(out_ref.dtype)


def tile_sums(which, lists, counts, near, far, vals, dtype):
    rows = near.shape[1]
    smem = pl.BlockSpec(memory_space=pltpu.SMEM)
    vmem = pl.BlockSpec(memory_space=pltpu.VMEM)
    return pl.pallas_call(
        lambda *refs: tile_kernel(which, *refs),
        out_shape=jax.ShapeDtypeStruct((BLOCK, rows, BLOCK), dtype),
        in_specs=[smem, smem, vmem, vmem, pl.BlockSpec(memory_space=pl.ANY)],
        out_specs=vmem,
        scratch_shapes=[
            pltpu.VMEM((BLOCK + 1, rows, BLOCK), jnp.float32),
            pltpu.VMEM((16, rows, BLOCK), jnp.bfloat16),
            pltpu.VMEM((DEPTH * GROUP, BLOCK, BLOCK), jnp.bfloat16),
            pltpu.SemaphoreType.DMA((DEPTH,)),
        ],
        compiler_params=pltpu.CompilerParams(vmem_limit_bytes=24 * 1024 * 1024),
        cost_estimate=pl.CostEstimate(flops=2 * 128 * rows * 128 * 128, bytes_accessed=8 << 20, transcendentals=0),
    )(lists, counts, near, far, vals)


def half16(x):
    return x.astype(jnp.bfloat16)


def wide(x):
    return x.astype(jnp.float32)


def reduce_blocks(keep):
    first, second, third, fourth = (keep[32 * g : 32 * g + 32].reshape(2, 2, 4, 2, *keep.shape[1:]) for g in range(4))
    came_first = lax.ppermute(half16(first[1]), "z", EVEN_PAIRS)
    came_second = lax.ppermute(half16(second[1]), "z", ODD_PAIRS)
    late = jnp.concatenate([third, fourth], axis=3)
    came_late = lax.ppermute(half16(late[1]), "pair", swap(2))
    early = jnp.concatenate([first[0] + wide(came_first), second[0] + wide(came_second)], axis=2)
    late = late[0] + wide(came_late)
    came_early = lax.ppermute(half16(early[1]), "pair", swap(2))
    came_third = lax.ppermute(half16(late[1, :, :2]), "z", EVEN_PAIRS)
    came_fourth = lax.ppermute(half16(late[1, :, 2:]), "z", ODD_PAIRS)
    early = early[0] + wide(came_early)
    late = jnp.concatenate([late[0, :, :2] + wide(came_third), late[0, :, 2:] + wide(came_fourth)], axis=1)
    both = jnp.concatenate([early, late], axis=1)
    rounded = half16(both)
    total = both[0]
    for k in (1, 3, 2):
        total = total + wide(lax.ppermute(rounded[k], "z", turn(2 * k, 8)))
    return total


def reduce_weights(grads):
    halves = (("core", lax.axis_index("core")), ("pair", lax.axis_index("pair")), ("half", lax.axis_index("half")))
    part = grads
    for axis, me in halves:
        n = part.shape[0] // 2
        mine = lax.dynamic_slice_in_dim(part, me * n, n, 0)
        other = lax.dynamic_slice_in_dim(part, (1 - me) * n, n, 0)
        part = mine + lax.ppermute(other, axis, swap(2))
    for k in (1, 2, 4):
        part = part + lax.ppermute(part, "z", [(i, i ^ k) for i in range(8)])
    for axis, me in reversed(halves):
        came = lax.ppermute(part, axis, swap(2))
        part = jnp.where(me == 0, jnp.concatenate([part, came]), jnp.concatenate([came, part]))
    return part


def contract_nodes(left, right):
    return lax.dot_general(left, right, (((1,), (1,)), ((), ())), preferred_element_type=jnp.float32)


def on_device(
    cotangent, preact, features, aggregated, w_self, w_neigh, tile_rows, tile_cols, tile_vals, tile_live
):
    z, pair, core, half, x = (lax.axis_index(a) for a in AXES)
    delta = jnp.where(preact > 0, cotangent, jnp.zeros_like(cotangent))
    rows, nodes = delta.shape
    in_width = w_self.shape[0]

    grads = reduce_weights(
        jnp.concatenate([contract_nodes(features, delta), contract_nodes(aggregated, delta)], axis=0)
    )

    hidden = [delta] + [lax.ppermute(delta, "x", turn(k, 4)) for k in (1, 2, 3)]
    weights = jnp.concatenate(
        [lax.dynamic_slice_in_dim(w, x * rows, rows, 0) for w in (w_neigh, w_self)], axis=0
    )
    weights = jnp.concatenate(
        [lax.dynamic_slice_in_dim(weights, (x + 4 - k) % 4 * rows, rows, 1) for k in range(4)], axis=1
    )
    both = jnp.dot(weights, jnp.concatenate(hidden, axis=0), preferred_element_type=jnp.float32)
    near = half16(both[:rows]).reshape(rows, nodes // BLOCK, BLOCK).transpose(1, 0, 2)
    far = lax.ppermute(near, "half", swap(2))
    self_term = both[rows:]

    slots = jnp.arange(tile_rows.shape[0], dtype=jnp.int32)
    owner, within = tile_cols // 16, tile_cols % 8
    group = within // 2
    shift = group % 2
    at, me = (owner // 4 + shift) % 8, (z + shift) % 8
    step = (at % 2) ^ (me % 2)
    turns = (at // 2 - me // 2 + 4) % 4
    across = (owner // 2 % 2) ^ pair
    outer = jnp.where(group < 2, step, across)
    inner = jnp.where(group < 2, across, step)
    place = group * 32 + ((outer * 2 + inner) * 4 + turns) * 2 + within % 2
    block = (tile_rows - (z * 4 + pair * 2 + core) * 16) ^ (half * 8)
    lists, counts = make_lists(
        tile_live, slots * 65536 + block * 256 + place, 1 - ((owner % 2) ^ core).astype(jnp.int32)
    )

    away = tile_sums(0, lists, counts, near, far, tile_vals, jnp.bfloat16)
    came = lax.ppermute(away, "core", swap(2))
    keep = tile_sums(1, lists, counts, near, far, tile_vals, jnp.float32)
    summed = reduce_blocks(keep + wide(came))
    summed = summed.transpose(1, 0, 2).reshape(rows, nodes)
    input_grad = half16(summed + self_term)
    return (input_grad, grads[:in_width], grads[in_width:])


def solution(mesh):
    nodes = ("z", "pair", "core", "half")
    return jax.shard_map(
        on_device,
        mesh=Mesh(mesh.devices.reshape(8, 2, 2, 2, 4), AXES),
        in_specs=(
            P("x", nodes),
            P("x", nodes),
            P(None, nodes),
            P(None, nodes),
            P(),
            P(),
            P(nodes),
            P(nodes),
            P(nodes, None, None),
            P(nodes),
        ),
        out_specs=(P("x", nodes), P(None, "x"), P(None, "x")),
        check_vma=False,
    )
```

```python
import jax
import jax.numpy as jnp
from jax import lax
from jax.experimental import pallas as pl
from jax.experimental.pallas import tpu as pltpu
from jax.sharding import Mesh, PartitionSpec as P

AXES = ("z", "pair", "core", "half", "x")
BLOCK = 128
GROUP = 8
BIG = 32
LISTS = 2
PLACES = 128
ROOM = 256 + LISTS * GROUP
SCOPED = 16 * 1024 * 1024


def swap(n):
    return [(i, i ^ 1) for i in range(n)]


def turn(k, n):
    return [(i, (i + k) % n) for i in range(n)]


EVEN_PAIRS = swap(8)
ODD_PAIRS = [(i, (((i + 1) % 8 ^ 1) - 1) % 8) for i in range(8)]


def list_kernel(table_ref, vals_ref, lists_ref, starts_ref, tiles_ref, sem):
    slots = vals_ref.shape[0]
    steps = (table_ref[2 * slots + LISTS + 1] + GROUP - 1) // GROUP
    starts_ref[0] = table_ref[2 * slots]
    for i in range(1, LISTS + 1):
        end = table_ref[2 * slots + i]
        starts_ref[i] = end
        for k in range(GROUP - 1):
            lists_ref[jnp.maximum(end - 1 - k, 0)] = jnp.int32(PLACES)

    def place(step, carry):
        for k in range(GROUP):
            slot = step * GROUP + k
            spot = table_ref[slot]
            lists_ref[spot] = table_ref[slots + slot]
            pltpu.make_async_copy(vals_ref.at[slot], tiles_ref.at[spot], sem).start()
        return carry

    def finish(step, carry):
        some = pl.ds(0, GROUP)
        pltpu.make_async_copy(vals_ref.at[some], tiles_ref.at[some], sem).wait()
        return carry

    lax.fori_loop(0, steps, place, 0)
    lax.fori_loop(0, steps, finish, 0)


def make_lists(live, entries, which, vals):
    slots = jnp.arange(vals.shape[0], dtype=jnp.int32)
    which = jnp.where(slots < live, which, LISTS)
    earlier = (which[:, None] == which[None, :]) & (slots[:, None] > slots[None, :])
    rank = jnp.sum(earlier.astype(jnp.int32), axis=1)
    starts = [jnp.int32(0)]
    for i in range(LISTS):
        held = jnp.sum((which == i).astype(jnp.int32))
        starts.append(starts[-1] + (held + GROUP - 1) // GROUP * GROUP)
    spots = ROOM + slots % GROUP
    for i in range(LISTS):
        spots = jnp.where(which == i, starts[i] + rank, spots)
    table = jnp.concatenate([spots, entries, jnp.stack(starts + [live])])
    smem = pl.BlockSpec(memory_space=pltpu.SMEM)
    return pl.pallas_call(
        list_kernel,
        out_shape=(
            pltpu.SMEM((ROOM + GROUP,), jnp.int32),
            pltpu.SMEM((LISTS + 1,), jnp.int32),
            pltpu.VMEM((ROOM + GROUP, BLOCK, BLOCK), vals.dtype),
        ),
        in_specs=[smem, pl.BlockSpec(memory_space=pl.ANY)],
        out_specs=(smem, smem, pl.BlockSpec(memory_space=pltpu.VMEM)),
        scratch_shapes=[pltpu.SemaphoreType.DMA],
        compiler_params=pltpu.CompilerParams(vmem_limit_bytes=SCOPED),
        cost_estimate=pl.CostEstimate(flops=0, bytes_accessed=12 << 20, transcendentals=0),
    )(table, pltpu.with_memory_space_constraint(vals, pltpu.HBM))


def tile_kernel(which, lists_ref, starts_ref, near_ref, far_ref, tiles_ref, first_ref, last_ref, total, panel):
    start, end = starts_ref[which], starts_ref[which + 1]
    panel[0:8] = near_ref[...]
    panel[8:16] = far_ref[...]
    total[...] = jnp.zeros_like(total)

    def add(base, count):
        entries = [lists_ref[base + k] for k in range(count)]
        products = [
            jnp.dot(panel[entry // 256], tiles_ref[base + k], preferred_element_type=jnp.float32)
            for k, entry in enumerate(entries)
        ]
        for entry, product in zip(entries, products):
            total[entry & 255] += product

    def big(step, carry):
        add(start + step * BIG, BIG)
        return carry

    def small(step, carry):
        add(start + step * GROUP, GROUP)
        return carry

    bigs = (end - start) // BIG
    lax.fori_loop(0, bigs, big, 0)
    lax.fori_loop(bigs * (BIG // GROUP), (end - start) // GROUP, small, 0)
    n = PLACES // 2
    first_ref[...] = total[0:n].astype(first_ref.dtype)
    last_ref[...] = total[n : 2 * n].astype(last_ref.dtype)


def tile_sums(which, lists, starts, near, far, tiles, dtype):
    rows = near.shape[1]
    smem = pl.BlockSpec(memory_space=pltpu.SMEM)
    vmem = pl.BlockSpec(memory_space=pltpu.VMEM)
    return pl.pallas_call(
        lambda *refs: tile_kernel(which, *refs),
        out_shape=(jax.ShapeDtypeStruct((PLACES // 2, rows, BLOCK), dtype),) * 2,
        in_specs=[smem, smem, vmem, vmem, vmem],
        out_specs=(vmem, vmem),
        scratch_shapes=[
            pltpu.VMEM((PLACES + 1, rows, BLOCK), jnp.float32),
            pltpu.VMEM((16, rows, BLOCK), jnp.bfloat16),
        ],
        compiler_params=pltpu.CompilerParams(vmem_limit_bytes=SCOPED),
        cost_estimate=pl.CostEstimate(flops=2 * 64 * rows * 128 * 128, bytes_accessed=4 << 20, transcendentals=0),
    )(
        pltpu.with_memory_space_constraint(lists, pltpu.SMEM),
        pltpu.with_memory_space_constraint(starts, pltpu.SMEM),
        near,
        far,
        pltpu.with_memory_space_constraint(tiles, pltpu.VMEM),
    )


def half16(x):
    return x.astype(jnp.bfloat16)


def wide(x):
    return x.astype(jnp.float32)


def under(core_sum, shape):
    return core_sum.reshape(*shape, *core_sum.shape[1:])


def weight_steps():
    def give(axis):
        me = lax.axis_index(axis)

        def step(part):
            n = part.shape[0] // 2
            mine = lax.dynamic_slice_in_dim(part, me * n, n, 0)
            other = lax.dynamic_slice_in_dim(part, (1 - me) * n, n, 0)
            return mine + lax.ppermute(other, axis, swap(2))

        return step

    def join(axis, k):
        return lambda part: part + lax.ppermute(part, axis, [(i, i ^ k) for i in range(lax.axis_size(axis))])

    def collect(axis):
        me = lax.axis_index(axis)

        def step(part):
            came = lax.ppermute(part, axis, swap(2))
            return jnp.where(me == 0, jnp.concatenate([part, came]), jnp.concatenate([came, part]))

        return step

    return iter(
        [give("core"), join("z", 1), join("z", 2), join("z", 4), join("pair", 1), join("half", 1), collect("core")]
    )


def beside(steps, count, part, *others):
    for _ in range(count):
        part = next(steps)(part)
    return lax.optimization_barrier((part, *others))


def contract_nodes(left, right):
    return lax.dot_general(left, right, (((1,), (1,)), ((), ())), preferred_element_type=jnp.float32)


def on_device(
    cotangent, preact, features, aggregated, w_self, w_neigh, tile_rows, tile_cols, tile_vals, tile_live
):
    z, pair, core, half, x = (lax.axis_index(a) for a in AXES)
    delta = jnp.where(preact > 0, cotangent, jnp.zeros_like(cotangent))
    rows, nodes = delta.shape
    in_width = w_self.shape[0]

    steps = weight_steps()
    part = jnp.concatenate([contract_nodes(features, delta), contract_nodes(aggregated, delta)], axis=0)
    hidden = [lax.ppermute(delta, "x", turn(k, 4)) for k in (1, 2, 3)]
    part, *hidden = beside(steps, 1, part, *hidden)
    hidden = [delta] + hidden
    weights = jnp.concatenate(
        [lax.dynamic_slice_in_dim(w, x * rows, rows, 0) for w in (w_neigh, w_self)], axis=0
    )
    weights = jnp.concatenate(
        [lax.dynamic_slice_in_dim(weights, (x + 4 - k) % 4 * rows, rows, 1) for k in range(4)], axis=1
    )
    both = jnp.dot(weights, jnp.concatenate(hidden, axis=0), preferred_element_type=jnp.float32)
    near = half16(both[:rows]).reshape(rows, nodes // BLOCK, BLOCK).transpose(1, 0, 2)
    part, near = lax.optimization_barrier((part, near))
    far = lax.ppermute(near, "half", swap(2))
    part, far = beside(steps, 1, part, far)
    self_term = both[rows:]

    owner, within = tile_cols // 16, tile_cols % 8
    late, odd = within // 4, within // 2 % 2
    at, me = (owner // 4 + odd) % 8, (z + odd) % 8
    step = (at % 2) ^ (me % 2)
    turns = (at // 2 - me // 2 + 4) % 4
    across = (owner // 2 % 2) ^ pair
    place = jnp.where(late == 1, (across * 2 + odd) * 2 + step, (step * 2 + odd) * 2 + across)
    place = ((1 - late) * 8 + place) * 8 + turns * 2 + within % 2
    block = (tile_rows - (z * 4 + pair * 2 + core) * 16) ^ (half * 8)
    which = 1 - ((owner % 2) ^ core).astype(jnp.int32)
    lists, starts, tiles = make_lists(tile_live[0], block * 256 + place, which, tile_vals)

    away_late, away_early = tile_sums(0, lists, starts, near, far, tiles, jnp.bfloat16)
    came_late = lax.ppermute(away_late, "core", swap(2))
    came_early = lax.ppermute(away_early, "core", swap(2))
    late, early = tile_sums(1, lists, starts, near, far, tiles, jnp.float32)
    late = under(late + wide(came_late), (2, 2, 2, 4, 2))
    came_late = lax.ppermute(half16(late[1]), "pair", swap(2))
    early = under(early + wide(came_early), (2, 2, 2, 4, 2))
    even, odd_ones = half16(early[1, 0]), half16(early[1, 1])
    part, even, odd_ones = beside(steps, 1, part, even, odd_ones)
    came_even = lax.ppermute(even, "z", EVEN_PAIRS)
    came_odd = lax.ppermute(odd_ones, "z", ODD_PAIRS)
    part, came_even, came_odd, came_late = beside(steps, 1, part, came_even, came_odd, came_late)

    early = early[0] + wide(jnp.stack([came_even, came_odd]))
    late = late[0] + wide(came_late)
    across, even, odd_ones = half16(early[:, 1]), half16(late[0, 1]), half16(late[1, 1])
    part, across, even, odd_ones = lax.optimization_barrier((part, across, even, odd_ones))
    came_early = lax.ppermute(across, "pair", swap(2))
    came_even = lax.ppermute(even, "z", EVEN_PAIRS)
    came_odd = lax.ppermute(odd_ones, "z", ODD_PAIRS)
    part, came_early, came_even, came_odd = beside(steps, 1, part, came_early, came_even, came_odd)

    early = early[:, 0] + wide(came_early)
    late = late[:, 0] + wide(jnp.stack([came_even, came_odd]))
    both = jnp.concatenate([early, late], axis=0)
    rounded = half16(both)
    came = [lax.ppermute(rounded[:, k], "z", turn(2 * k, 8)) for k in (1, 3, 2)]
    part, came[0] = lax.optimization_barrier((part, came[0]))
    for step in steps:
        part = step(part)
    summed = both[:, 0] + wide(came[0]) + wide(came[1]) + wide(came[2])
    summed = summed.reshape(8, rows, BLOCK).transpose(1, 0, 2).reshape(rows, nodes)
    input_grad = half16(summed + self_term)
    return (input_grad, part[:in_width], part[in_width:])


def solution(mesh):
    nodes = ("z", "pair", "core", "half")
    return jax.shard_map(
        on_device,
        mesh=Mesh(mesh.devices.reshape(8, 2, 2, 2, 4), AXES),
        in_specs=(
            P("x", nodes),
            P("x", nodes),
            P(None, nodes),
            P(None, nodes),
            P(),
            P(),
            P(nodes),
            P(nodes),
            P(nodes, None, None),
            P(nodes),
        ),
        out_specs=(P("x", nodes), P(None, "x"), P(None, "x")),
        check_vma=False,
    )
```

```python
import jax
import jax.numpy as jnp
from jax import lax
from jax.experimental import pallas as pl
from jax.experimental.pallas import tpu as pltpu
from jax.sharding import Mesh, PartitionSpec as P

AXES = ("z", "pair", "core", "half", "x")
BLOCK = 128
GROUP = 8
BIG = 32
LISTS = 2
PLACES = 128
ROOM = 256 + LISTS * GROUP
SCOPED = 16 * 1024 * 1024


def swap(n):
    return [(i, i ^ 1) for i in range(n)]


def turn(k, n):
    return [(i, (i + k) % n) for i in range(n)]


EVEN_PAIRS = swap(8)
ODD_PAIRS = [(i, (((i + 1) % 8 ^ 1) - 1) % 8) for i in range(8)]


def list_kernel(table_ref, vals_ref, lists_ref, starts_ref, tiles_ref, sem):
    slots = vals_ref.shape[0]
    steps = (table_ref[2 * slots + LISTS + 1] + GROUP - 1) // GROUP
    starts_ref[0] = table_ref[2 * slots]
    for i in range(1, LISTS + 1):
        end = table_ref[2 * slots + i]
        starts_ref[i] = end
        for k in range(GROUP - 1):
            lists_ref[jnp.maximum(end - 1 - k, 0)] = jnp.int32(PLACES)

    def place(step, carry):
        for k in range(GROUP):
            slot = step * GROUP + k
            spot = table_ref[slot]
            lists_ref[spot] = table_ref[slots + slot]
            pltpu.make_async_copy(vals_ref.at[slot], tiles_ref.at[spot], sem).start()
        return carry

    def finish(step, carry):
        some = pl.ds(0, GROUP)
        pltpu.make_async_copy(vals_ref.at[some], tiles_ref.at[some], sem).wait()
        return carry

    lax.fori_loop(0, steps, place, 0)
    lax.fori_loop(0, steps, finish, 0)


def make_lists(live, entries, which, vals):
    slots = jnp.arange(vals.shape[0], dtype=jnp.int32)
    which = jnp.where(slots < live, which, LISTS)
    earlier = (which[:, None] == which[None, :]) & (slots[:, None] > slots[None, :])
    rank = jnp.sum(earlier.astype(jnp.int32), axis=1)
    starts = [jnp.int32(0)]
    for i in range(LISTS):
        held = jnp.sum((which == i).astype(jnp.int32))
        starts.append(starts[-1] + (held + GROUP - 1) // GROUP * GROUP)
    spots = ROOM + slots % GROUP
    for i in range(LISTS):
        spots = jnp.where(which == i, starts[i] + rank, spots)
    table = jnp.concatenate([spots, entries, jnp.stack(starts + [live])])
    smem = pl.BlockSpec(memory_space=pltpu.SMEM)
    return pl.pallas_call(
        list_kernel,
        out_shape=(
            pltpu.SMEM((ROOM + GROUP,), jnp.int32),
            pltpu.SMEM((LISTS + 1,), jnp.int32),
            pltpu.VMEM((ROOM + GROUP, BLOCK, BLOCK), vals.dtype),
        ),
        in_specs=[smem, pl.BlockSpec(memory_space=pl.ANY)],
        out_specs=(smem, smem, pl.BlockSpec(memory_space=pltpu.VMEM)),
        scratch_shapes=[pltpu.SemaphoreType.DMA],
        compiler_params=pltpu.CompilerParams(vmem_limit_bytes=SCOPED),
        cost_estimate=pl.CostEstimate(flops=0, bytes_accessed=12 << 20, transcendentals=0),
    )(table, pltpu.with_memory_space_constraint(vals, pltpu.HBM))


def tile_kernel(which, lists_ref, starts_ref, near_ref, far_ref, tiles_ref, first_ref, last_ref, total, panel):
    start, end = starts_ref[which], starts_ref[which + 1]
    panel[0:8] = near_ref[...]
    panel[8:16] = far_ref[...]
    total[...] = jnp.zeros_like(total)

    def add(base, count):
        entries = [lists_ref[base + k] for k in range(count)]
        products = [
            jnp.dot(panel[entry // 256], tiles_ref[base + k], preferred_element_type=jnp.float32)
            for k, entry in enumerate(entries)
        ]
        for entry, product in zip(entries, products):
            total[entry & 255] += product

    def big(step, carry):
        add(start + step * BIG, BIG)
        return carry

    def small(step, carry):
        add(start + step * GROUP, GROUP)
        return carry

    bigs = (end - start) // BIG
    lax.fori_loop(0, bigs, big, 0)
    lax.fori_loop(bigs * (BIG // GROUP), (end - start) // GROUP, small, 0)
    n = PLACES // 2
    first_ref[...] = total[0:n].astype(first_ref.dtype)
    last_ref[...] = total[n : 2 * n].astype(last_ref.dtype)


def tile_sums(which, lists, starts, near, far, tiles, dtype):
    rows = near.shape[1]
    smem = pl.BlockSpec(memory_space=pltpu.SMEM)
    vmem = pl.BlockSpec(memory_space=pltpu.VMEM)
    return pl.pallas_call(
        lambda *refs: tile_kernel(which, *refs),
        out_shape=(jax.ShapeDtypeStruct((PLACES // 2, rows, BLOCK), dtype),) * 2,
        in_specs=[smem, smem, vmem, vmem, vmem],
        out_specs=(vmem, vmem),
        scratch_shapes=[
            pltpu.VMEM((PLACES + 1, rows, BLOCK), jnp.float32),
            pltpu.VMEM((16, rows, BLOCK), jnp.bfloat16),
        ],
        compiler_params=pltpu.CompilerParams(vmem_limit_bytes=SCOPED),
        cost_estimate=pl.CostEstimate(flops=2 * 64 * rows * 128 * 128, bytes_accessed=4 << 20, transcendentals=0),
    )(
        pltpu.with_memory_space_constraint(lists, pltpu.SMEM),
        pltpu.with_memory_space_constraint(starts, pltpu.SMEM),
        near,
        far,
        pltpu.with_memory_space_constraint(tiles, pltpu.VMEM),
    )


def half16(x):
    return x.astype(jnp.bfloat16)


def wide(x):
    return x.astype(jnp.float32)


def under(core_sum, shape):
    return core_sum.reshape(*shape, *core_sum.shape[1:])


def weight_steps():
    def give(axis):
        me = lax.axis_index(axis)

        def step(part):
            n = part.shape[0] // 2
            mine = lax.dynamic_slice_in_dim(part, me * n, n, 0)
            other = lax.dynamic_slice_in_dim(part, (1 - me) * n, n, 0)
            return mine + lax.ppermute(other, axis, swap(2))

        return step

    def join(axis, k):
        return lambda part: part + lax.ppermute(part, axis, [(i, i ^ k) for i in range(lax.axis_size(axis))])

    return iter(
        [give("core"), join("z", 1), join("z", 4), join("z", 2), join("pair", 1), join("half", 1)]
    )


def beside(steps, count, part, *others):
    for _ in range(count):
        part = next(steps)(part)
    return lax.optimization_barrier((part, *others))


def contract_nodes(left, right):
    return lax.dot_general(left, right, (((1,), (1,)), ((), ())), preferred_element_type=jnp.float32)


def on_device(
    cotangent, preact, features, aggregated, w_self, w_neigh, tile_rows, tile_cols, tile_vals, tile_live
):
    z, pair, core, half, x = (lax.axis_index(a) for a in AXES)
    delta = jnp.where(preact > 0, cotangent, jnp.zeros_like(cotangent))
    rows, nodes = delta.shape

    steps = weight_steps()
    part = jnp.concatenate([contract_nodes(features, delta), contract_nodes(aggregated, delta)], axis=0)
    hidden = [lax.ppermute(delta, "x", turn(k, 4)) for k in (1, 2, 3)]
    part, *hidden = beside(steps, 1, part, *hidden)
    hidden = [delta] + hidden
    weights = jnp.concatenate(
        [lax.dynamic_slice_in_dim(w, x * rows, rows, 0) for w in (w_neigh, w_self)], axis=0
    )
    weights = jnp.concatenate(
        [lax.dynamic_slice_in_dim(weights, (x + 4 - k) % 4 * rows, rows, 1) for k in range(4)], axis=1
    )
    both = jnp.dot(weights, jnp.concatenate(hidden, axis=0), preferred_element_type=jnp.float32)
    near = half16(both[:rows]).reshape(rows, nodes // BLOCK, BLOCK).transpose(1, 0, 2)
    part, near = lax.optimization_barrier((part, near))
    far = lax.ppermute(near, "half", swap(2))
    part, far = beside(steps, 1, part, far)
    self_term = both[rows:]

    owner, within = tile_cols // 16, tile_cols % 8
    late, odd = within // 4, within // 2 % 2
    at, me = (owner // 4 + odd) % 8, (z + odd) % 8
    step = (at % 2) ^ (me % 2)
    turns = (at // 2 - me // 2 + 4) % 4
    across = (owner // 2 % 2) ^ pair
    place = jnp.where(late == 1, (across * 2 + odd) * 2 + step, (step * 2 + odd) * 2 + across)
    place = ((1 - late) * 8 + place) * 8 + turns * 2 + within % 2
    block = (tile_rows - (z * 4 + pair * 2 + core) * 16) ^ (half * 8)
    which = 1 - ((owner % 2) ^ core).astype(jnp.int32)
    lists, starts, tiles = make_lists(tile_live[0], block * 256 + place, which, tile_vals)

    away_late, away_early = tile_sums(0, lists, starts, near, far, tiles, jnp.bfloat16)
    came_late = lax.ppermute(away_late, "core", swap(2))
    came_early = lax.ppermute(away_early, "core", swap(2))
    late, early = tile_sums(1, lists, starts, near, far, tiles, jnp.float32)
    late = under(late + wide(came_late), (2, 2, 2, 4, 2))
    came_late = lax.ppermute(half16(late[1]), "pair", swap(2))
    early = under(early + wide(came_early), (2, 2, 2, 4, 2))
    even, odd_ones = half16(early[1, 0]), half16(early[1, 1])
    part, even, odd_ones = lax.optimization_barrier((part, even, odd_ones))
    came_even = lax.ppermute(even, "z", EVEN_PAIRS)
    came_odd = lax.ppermute(odd_ones, "z", ODD_PAIRS)
    part, came_even, came_odd, came_late = beside(steps, 1, part, came_even, came_odd, came_late)

    early = early[0] + wide(jnp.stack([came_even, came_odd]))
    late = late[0] + wide(came_late)
    across, even, odd_ones = half16(early[:, 1]), half16(late[0, 1]), half16(late[1, 1])
    part, across, even, odd_ones = lax.optimization_barrier((part, across, even, odd_ones))
    came_early = lax.ppermute(across, "pair", swap(2))
    came_even = lax.ppermute(even, "z", EVEN_PAIRS)
    came_odd = lax.ppermute(odd_ones, "z", ODD_PAIRS)
    part, came_early, came_even, came_odd = beside(steps, 1, part, came_early, came_even, came_odd)

    early = early[:, 0] + wide(came_early)
    late = late[:, 0] + wide(jnp.stack([came_even, came_odd]))
    both = jnp.concatenate([early, late], axis=0)
    rounded = half16(both)
    part, rounded = lax.optimization_barrier((part, rounded))
    came = [lax.ppermute(rounded[:, k], "z", turn(2 * k, 8)) for k in (1, 3, 2)]
    part = next(steps)(next(steps)(part))
    other = lax.ppermute(part, "core", swap(2))
    grads = jnp.where(core == 0, part, other), jnp.where(core == 0, other, part)
    summed = both[:, 0] + wide(came[0]) + wide(came[1]) + wide(came[2])
    summed = summed.reshape(8, rows, BLOCK).transpose(1, 0, 2).reshape(rows, nodes)
    input_grad = half16(summed + self_term)
    return (input_grad, *grads)


def solution(mesh):
    nodes = ("z", "pair", "core", "half")
    return jax.shard_map(
        on_device,
        mesh=Mesh(mesh.devices.reshape(8, 2, 2, 2, 4), AXES),
        in_specs=(
            P("x", nodes),
            P("x", nodes),
            P(None, nodes),
            P(None, nodes),
            P(),
            P(),
            P(nodes),
            P(nodes),
            P(nodes, None, None),
            P(nodes),
        ),
        out_specs=(P("x", nodes), P(None, "x"), P(None, "x")),
        check_vma=False,
    )
```

```python
import jax
import jax.numpy as jnp
from jax import lax
from jax.experimental import pallas as pl
from jax.experimental.pallas import tpu as pltpu
from jax.sharding import Mesh, PartitionSpec as P

AXES = ("z", "pair", "core", "half", "x")
BLOCK = 128
GROUP = 16
BIG = 64
CHUNK = 32
LISTS = 3
PLACES = 64
ROOM = 256 + LISTS * GROUP
SCOPED = 16 * 1024 * 1024


def swap(n):
    return [(i, i ^ 1) for i in range(n)]


def turn(k, n):
    return [(i, (i + k) % n) for i in range(n)]


EVEN_PAIRS = swap(8)
ODD_PAIRS = [(i, (((i + 1) % 8 ^ 1) - 1) % 8) for i in range(8)]


def list_kernel(table_ref, vals_ref, lists_ref, starts_ref, tiles_ref, sem):
    slots = vals_ref.shape[0]
    live = table_ref[2 * slots + 8]
    chunks = (live + CHUNK - 1) // CHUNK

    def fetch(chunk, carry):
        some = pl.ds(chunk * CHUNK, CHUNK)
        pltpu.make_async_copy(vals_ref.at[some], tiles_ref.at[some], sem).start()
        return carry

    lax.fori_loop(0, chunks, fetch, 0)
    starts_ref[0] = table_ref[2 * slots]
    for i in range(1, LISTS + 1):
        end = table_ref[2 * slots + i]
        starts_ref[i] = end
        for k in range(GROUP - 1):
            lists_ref[jnp.maximum(end - 1 - k, 0)] = jnp.int32(2 * PLACES)

    def place(step, carry):
        for k in range(GROUP):
            slot = step * GROUP + k
            lists_ref[table_ref[slot]] = table_ref[slots + slot]
        return carry

    def finish(chunk, carry):
        some = pl.ds(0, CHUNK)
        pltpu.make_async_copy(vals_ref.at[some], tiles_ref.at[some], sem).wait()
        return carry

    lax.fori_loop(0, (live + GROUP - 1) // GROUP, place, 0)
    lax.fori_loop(0, chunks, finish, 0)


def list_table(live, entries, which):
    slots = jnp.arange(entries.shape[0], dtype=jnp.int32)
    which = jnp.where(slots < live, which, LISTS)
    earlier = (which[:, None] == which[None, :]) & (slots[:, None] > slots[None, :])
    rank = jnp.sum(earlier.astype(jnp.int32), axis=1)
    lists = jnp.arange(8, dtype=jnp.int32)
    member = which[:, None] == lists[None, :]
    held = jnp.sum(member.astype(jnp.int32), axis=0)
    room = (held + GROUP - 1) // GROUP * GROUP
    starts = jnp.sum(jnp.where(lists[:, None] < lists[None, :], room[:, None], 0), axis=0)
    first = jnp.sum(jnp.where(member, starts[None, :], 0), axis=1)
    spots = jnp.where(which < LISTS, first + rank, ROOM + slots % GROUP)
    return jnp.concatenate([spots, slots * 65536 + entries, starts, live])


def make_lists(table, vals):
    smem = pl.BlockSpec(memory_space=pltpu.SMEM)
    return pl.pallas_call(
        list_kernel,
        out_shape=(
            pltpu.SMEM((ROOM + GROUP,), jnp.int32),
            pltpu.SMEM((LISTS + 1,), jnp.int32),
            pltpu.VMEM(vals.shape, vals.dtype),
        ),
        in_specs=[smem, pl.BlockSpec(memory_space=pl.ANY)],
        out_specs=(smem, smem, pl.BlockSpec(memory_space=pltpu.VMEM)),
        scratch_shapes=[pltpu.SemaphoreType.DMA],
        compiler_params=pltpu.CompilerParams(vmem_limit_bytes=SCOPED),
        cost_estimate=pl.CostEstimate(flops=0, bytes_accessed=12 << 20, transcendentals=0),
    )(table, pltpu.with_memory_space_constraint(vals, pltpu.HBM))


def tile_kernel(which, lists_ref, starts_ref, near_ref, far_ref, tiles_ref, *refs):
    *outs, total, panel = refs
    start, end = starts_ref[which], starts_ref[which + 1]
    panel[0:8] = near_ref[...]
    panel[8:16] = far_ref[...]
    used = len(outs) * PLACES
    total[0:used] = jnp.zeros((used, *total.shape[1:]), total.dtype)

    def add(base, count):
        entries = [lists_ref[base + k] for k in range(count)]
        products = [
            jnp.dot(panel[entry // 256 & 255], tiles_ref[entry // 65536], preferred_element_type=jnp.float32)
            for entry in entries
        ]
        for entry, product in zip(entries, products):
            total[entry & 255] += product

    def big(step, carry):
        add(start + step * BIG, BIG)
        return carry

    count = end - start
    lax.fori_loop(0, count // BIG, big, 0)
    size = BIG // 2
    while size >= GROUP:
        pl.when(count & size != 0)(lambda size=size: add(start + count // (2 * size) * (2 * size), size))
        size //= 2
    for i, out_ref in enumerate(outs):
        out_ref[...] = total[i * PLACES : (i + 1) * PLACES].astype(out_ref.dtype)


def tile_sums(which, outs, lists, starts, near, far, tiles, dtype):
    rows = near.shape[1]
    smem = pl.BlockSpec(memory_space=pltpu.SMEM)
    vmem = pl.BlockSpec(memory_space=pltpu.VMEM)
    return pl.pallas_call(
        lambda *refs: tile_kernel(which, *refs),
        out_shape=(jax.ShapeDtypeStruct((PLACES, rows, BLOCK), dtype),) * outs,
        in_specs=[smem, smem, vmem, vmem, vmem],
        out_specs=(vmem,) * outs,
        scratch_shapes=[
            pltpu.VMEM((2 * PLACES + 1, rows, BLOCK), jnp.float32),
            pltpu.VMEM((16, rows, BLOCK), jnp.bfloat16),
        ],
        compiler_params=pltpu.CompilerParams(vmem_limit_bytes=SCOPED),
        cost_estimate=pl.CostEstimate(flops=2 * 64 * rows * 128 * 128, bytes_accessed=4 << 20, transcendentals=0),
    )(
        pltpu.with_memory_space_constraint(lists, pltpu.SMEM),
        pltpu.with_memory_space_constraint(starts, pltpu.SMEM),
        near,
        far,
        pltpu.with_memory_space_constraint(tiles, pltpu.VMEM),
    )


def half16(x):
    return x.astype(jnp.bfloat16)


def wide(x):
    return x.astype(jnp.float32)


def under(core_sum, shape):
    return core_sum.reshape(*shape, *core_sum.shape[1:])


def weight_steps():
    def give(axis):
        me = lax.axis_index(axis)

        def step(part):
            n = part.shape[0] // 2
            mine = lax.dynamic_slice_in_dim(part, me * n, n, 0)
            other = lax.dynamic_slice_in_dim(part, (1 - me) * n, n, 0)
            return mine + lax.ppermute(other, axis, swap(2))

        return step

    def join(axis, k):
        return lambda part: part + lax.ppermute(part, axis, [(i, i ^ k) for i in range(lax.axis_size(axis))])

    return iter(
        [give("core"), join("z", 1), join("z", 4), join("z", 2), join("half", 1), join("pair", 1)]
    )


def beside(steps, count, part, *others):
    for _ in range(count):
        part = next(steps)(part)
    return lax.optimization_barrier((part, *others))


def contract_nodes(left, right):
    return lax.dot_general(left, right, (((1,), (1,)), ((), ())), preferred_element_type=jnp.float32)


def on_device(
    cotangent, preact, features, aggregated, w_self, w_neigh, tile_rows, tile_cols, tile_vals, tile_live
):
    z, pair, core, half, x = (lax.axis_index(a) for a in AXES)
    delta = jnp.where(preact > 0, cotangent, jnp.zeros_like(cotangent))
    rows, nodes = delta.shape

    steps = weight_steps()
    part = jnp.concatenate([contract_nodes(features, delta), contract_nodes(aggregated, delta)], axis=0)
    hidden = [lax.ppermute(delta, "x", turn(k, 4)) for k in (2, 3, 1)]
    part, *hidden = beside(steps, 1, part, *hidden)
    hidden = [delta] + hidden
    weights = jnp.concatenate(
        [lax.dynamic_slice_in_dim(w, x * rows, rows, 0) for w in (w_neigh, w_self)], axis=0
    )
    weights = jnp.concatenate(
        [lax.dynamic_slice_in_dim(weights, (x + 4 - k) % 4 * rows, rows, 1) for k in (0, 2, 3, 1)], axis=1
    )
    both = jnp.dot(weights, jnp.concatenate(hidden, axis=0), preferred_element_type=jnp.float32)
    near = half16(both[:rows]).reshape(rows, nodes // BLOCK, BLOCK).transpose(1, 0, 2)
    owner, within = tile_cols // 16, tile_cols % 8
    late, odd = within // 4, within // 2 % 2
    at, me = (owner // 4 + odd) % 8, (z + odd) % 8
    step = (at % 2) ^ (me % 2)
    turns = (at // 2 - me // 2 + 4) % 4
    across = (owner // 2 % 2) ^ pair
    place = jnp.where(late == 1, (across * 2 + odd) * 2 + step, (step * 2 + odd) * 2 + across)
    place = ((1 - late) * 8 + place) * 8 + turns * 2 + within % 2
    block = (tile_rows - (z * 4 + pair * 2 + core) * 16) ^ (half * 8)
    which = jnp.where((owner % 2) ^ core == 1, 1 - late, 2)
    place = place - jnp.where(which == 1, PLACES, 0)
    table = list_table(tile_live, block * 256 + place, which)

    table, _ = lax.optimization_barrier((table, near))
    part, table = lax.optimization_barrier((part, table))
    lists, starts, tiles = make_lists(table, tile_vals)
    far = lax.ppermute(near, "half", swap(2))
    part, far = beside(steps, 1, part, far)
    self_term = both[rows:]


    (away,) = tile_sums(0, 1, lists, starts, near, far, tiles, jnp.bfloat16)
    came_late = lax.ppermute(away, "core", swap(2))
    near, _ = lax.optimization_barrier((near, away))
    (away,) = tile_sums(1, 1, lists, starts, near, far, tiles, jnp.bfloat16)
    came_early = lax.ppermute(away, "core", swap(2))
    late, early = tile_sums(2, 2, lists, starts, near, far, tiles, jnp.float32)
    late = under(late + wide(came_late), (2, 2, 2, 4, 2))
    came_late = lax.ppermute(half16(late[1]), "pair", swap(2))
    early = under(early + wide(came_early), (2, 2, 2, 4, 2))
    even, odd_ones = half16(early[1, 0]), half16(early[1, 1])
    part, even, odd_ones = lax.optimization_barrier((part, even, odd_ones))
    came_even = lax.ppermute(even, "z", EVEN_PAIRS)
    came_odd = lax.ppermute(odd_ones, "z", ODD_PAIRS)
    part, came_even, came_odd, came_late = beside(steps, 1, part, came_even, came_odd, came_late)

    early = early[0] + wide(jnp.stack([came_even, came_odd]))
    late = late[0] + wide(came_late)
    across, even, odd_ones = half16(early[:, 1]), half16(late[0, 1]), half16(late[1, 1])
    part, across, even, odd_ones = lax.optimization_barrier((part, across, even, odd_ones))
    came_early = lax.ppermute(across, "pair", swap(2))
    came_even = lax.ppermute(even, "z", EVEN_PAIRS)
    came_odd = lax.ppermute(odd_ones, "z", ODD_PAIRS)
    part, came_early, came_even, came_odd = beside(steps, 1, part, came_early, came_even, came_odd)

    early = early[:, 0] + wide(came_early)
    late = late[:, 0] + wide(jnp.stack([came_even, came_odd]))
    both = jnp.concatenate([early, late], axis=0)
    rounded = half16(both)
    part, rounded = lax.optimization_barrier((part, rounded))
    came = [lax.ppermute(rounded[:, k], "z", turn(2 * k, 8)) for k in (1, 3, 2)]
    part = next(steps)(next(steps)(part))
    other = lax.ppermute(part, "core", swap(2))
    grads = jnp.where(core == 0, part, other), jnp.where(core == 0, other, part)
    summed = both[:, 0] + wide(came[0]) + wide(came[1]) + wide(came[2])
    summed = summed.reshape(8, rows, BLOCK).transpose(1, 0, 2).reshape(rows, nodes)
    input_grad = half16(summed + self_term)
    return (input_grad, *grads)


def solution(mesh):
    nodes = ("z", "pair", "core", "half")
    return jax.shard_map(
        on_device,
        mesh=Mesh(mesh.devices.reshape(8, 2, 2, 2, 4), AXES),
        in_specs=(
            P("x", nodes),
            P("x", nodes),
            P(None, nodes),
            P(None, nodes),
            P(),
            P(),
            P(nodes),
            P(nodes),
            P(nodes, None, None),
            P(nodes),
        ),
        out_specs=(P("x", nodes), P(None, "x"), P(None, "x")),
        check_vma=False,
    )
```

```python
import jax
import jax.numpy as jnp
from jax import lax
from jax.experimental import pallas as pl
from jax.experimental.pallas import tpu as pltpu
from jax.sharding import Mesh, PartitionSpec as P

AXES = ("z", "pair", "core", "half", "x")
BLOCK = 128
GROUP = 16
BIG = 64
CHUNK = 32
LISTS = 3
PLACES = 64
ROOM = 256 + LISTS * GROUP
SCOPED = 16 * 1024 * 1024


def swap(n):
    return [(i, i ^ 1) for i in range(n)]


def turn(k, n):
    return [(i, (i + k) % n) for i in range(n)]


EVEN_PAIRS = swap(8)
ODD_PAIRS = [(i, (((i + 1) % 8 ^ 1) - 1) % 8) for i in range(8)]


def list_kernel(table_ref, vals_ref, lists_ref, starts_ref, tiles_ref, sem):
    slots = vals_ref.shape[0]
    live = table_ref[2 * slots + 8]
    chunks = (live + CHUNK - 1) // CHUNK

    def fetch(chunk, carry):
        some = pl.ds(chunk * CHUNK, CHUNK)
        pltpu.make_async_copy(vals_ref.at[some], tiles_ref.at[some], sem).start()
        return carry

    lax.fori_loop(0, chunks, fetch, 0)
    starts_ref[0] = table_ref[2 * slots]
    for i in range(1, LISTS + 1):
        end = table_ref[2 * slots + i]
        starts_ref[i] = end
        for k in range(GROUP - 1):
            lists_ref[jnp.maximum(end - 1 - k, 0)] = jnp.int32(2 * PLACES)

    def place(step, carry):
        for k in range(GROUP):
            slot = step * GROUP + k
            lists_ref[table_ref[slot]] = table_ref[slots + slot]
        return carry

    def finish(chunk, carry):
        some = pl.ds(0, CHUNK)
        pltpu.make_async_copy(vals_ref.at[some], tiles_ref.at[some], sem).wait()
        return carry

    lax.fori_loop(0, (live + GROUP - 1) // GROUP, place, 0)
    lax.fori_loop(0, chunks, finish, 0)


def list_table(live, entries, which):
    slots = jnp.arange(entries.shape[0], dtype=jnp.int32)
    which = jnp.where(slots < live, which, LISTS)
    earlier = (which[:, None] == which[None, :]) & (slots[:, None] > slots[None, :])
    rank = jnp.sum(earlier.astype(jnp.int32), axis=1)
    lists = jnp.arange(8, dtype=jnp.int32)
    member = which[:, None] == lists[None, :]
    held = jnp.sum(member.astype(jnp.int32), axis=0)
    room = (held + GROUP - 1) // GROUP * GROUP
    starts = jnp.sum(jnp.where(lists[:, None] < lists[None, :], room[:, None], 0), axis=0)
    first = jnp.sum(jnp.where(member, starts[None, :], 0), axis=1)
    spots = jnp.where(which < LISTS, first + rank, ROOM + slots % GROUP)
    return jnp.concatenate([spots, slots * 65536 + entries, starts, live])


def make_lists(table, vals):
    smem = pl.BlockSpec(memory_space=pltpu.SMEM)
    return pl.pallas_call(
        list_kernel,
        out_shape=(
            pltpu.SMEM((ROOM + GROUP,), jnp.int32),
            pltpu.SMEM((LISTS + 1,), jnp.int32),
            pltpu.VMEM(vals.shape, vals.dtype),
        ),
        in_specs=[smem, pl.BlockSpec(memory_space=pl.ANY)],
        out_specs=(smem, smem, pl.BlockSpec(memory_space=pltpu.VMEM)),
        scratch_shapes=[pltpu.SemaphoreType.DMA],
        compiler_params=pltpu.CompilerParams(vmem_limit_bytes=SCOPED),
        cost_estimate=pl.CostEstimate(flops=0, bytes_accessed=12 << 20, transcendentals=0),
    )(table, pltpu.with_memory_space_constraint(vals, pltpu.HBM))


def tile_kernel(which, lists_ref, starts_ref, near_ref, far_ref, tiles_ref, *refs):
    *outs, total, panel = refs
    start, end = starts_ref[which], starts_ref[which + 1]
    panel[0:8] = near_ref[...]
    panel[8:16] = far_ref[...]
    used = len(outs) * PLACES
    total[0:used] = jnp.zeros((used, *total.shape[1:]), total.dtype)

    def add(base, count):
        entries = [lists_ref[base + k] for k in range(count)]
        products = [
            jnp.dot(panel[entry // 256 & 255], tiles_ref[entry // 65536], preferred_element_type=jnp.float32)
            for entry in entries
        ]
        for entry, product in zip(entries, products):
            total[entry & 255] += product

    def big(step, carry):
        add(start + step * BIG, BIG)
        return carry

    count = end - start
    lax.fori_loop(0, count // BIG, big, 0)
    size = BIG // 2
    while size >= GROUP:
        pl.when(count & size != 0)(lambda size=size: add(start + count // (2 * size) * (2 * size), size))
        size //= 2
    for i, out_ref in enumerate(outs):
        out_ref[...] = total[i * PLACES : (i + 1) * PLACES].astype(out_ref.dtype)


def tile_sums(which, outs, lists, starts, near, far, tiles, dtype):
    rows = near.shape[1]
    smem = pl.BlockSpec(memory_space=pltpu.SMEM)
    vmem = pl.BlockSpec(memory_space=pltpu.VMEM)
    return pl.pallas_call(
        lambda *refs: tile_kernel(which, *refs),
        out_shape=(jax.ShapeDtypeStruct((PLACES, rows, BLOCK), dtype),) * outs,
        in_specs=[smem, smem, vmem, vmem, vmem],
        out_specs=(vmem,) * outs,
        scratch_shapes=[
            pltpu.VMEM((2 * PLACES + 1, rows, BLOCK), jnp.float32),
            pltpu.VMEM((16, rows, BLOCK), jnp.bfloat16),
        ],
        compiler_params=pltpu.CompilerParams(vmem_limit_bytes=SCOPED),
        cost_estimate=pl.CostEstimate(flops=2 * 64 * rows * 128 * 128, bytes_accessed=4 << 20, transcendentals=0),
    )(
        pltpu.with_memory_space_constraint(lists, pltpu.SMEM),
        pltpu.with_memory_space_constraint(starts, pltpu.SMEM),
        near,
        far,
        pltpu.with_memory_space_constraint(tiles, pltpu.VMEM),
    )


def half16(x):
    return x.astype(jnp.bfloat16)


def wide(x):
    return x.astype(jnp.float32)


def under(core_sum, shape):
    return core_sum.reshape(*shape, *core_sum.shape[1:])


def weight_steps():
    def give(axis):
        me = lax.axis_index(axis)

        def step(part):
            n = part.shape[0] // 2
            mine = lax.dynamic_slice_in_dim(part, me * n, n, 0)
            other = lax.dynamic_slice_in_dim(part, (1 - me) * n, n, 0)
            return mine + lax.ppermute(other, axis, swap(2))

        return step

    def join(axis, k):
        return lambda part: part + lax.ppermute(part, axis, [(i, i ^ k) for i in range(lax.axis_size(axis))])

    return iter(
        [give("core"), join("z", 1), join("z", 4), join("z", 2), join("half", 1), join("pair", 1)]
    )


def beside(steps, count, part, *others):
    for _ in range(count):
        part = next(steps)(part)
    return lax.optimization_barrier((part, *others))


def contract_nodes(left, right):
    return lax.dot_general(left, right, (((1,), (1,)), ((), ())), preferred_element_type=jnp.float32)


def on_device(
    cotangent, preact, features, aggregated, w_self, w_neigh, tile_rows, tile_cols, tile_vals, tile_live
):
    z, pair, core, half, x = (lax.axis_index(a) for a in AXES)
    delta = jnp.where(preact > 0, cotangent, jnp.zeros_like(cotangent))
    rows, nodes = delta.shape

    steps = weight_steps()
    part = jnp.concatenate([contract_nodes(features, delta), contract_nodes(aggregated, delta)], axis=0)
    hidden = [lax.ppermute(delta, "x", turn(k, 4)) for k in (2, 3, 1)]
    part, *hidden = beside(steps, 1, part, *hidden)
    hidden = [delta] + hidden
    weights = jnp.concatenate(
        [lax.dynamic_slice_in_dim(w, x * rows, rows, 0) for w in (w_neigh, w_self)], axis=0
    )
    weights = jnp.concatenate(
        [lax.dynamic_slice_in_dim(weights, (x + 4 - k) % 4 * rows, rows, 1) for k in (0, 2, 3, 1)], axis=1
    )
    both = jnp.dot(weights, jnp.concatenate(hidden, axis=0), preferred_element_type=jnp.float32)
    near = half16(both[:rows]).reshape(rows, nodes // BLOCK, BLOCK).transpose(1, 0, 2)
    owner, within = tile_cols // 16, tile_cols % 8
    late, odd = within // 4, within // 2 % 2
    at, me = (owner // 4 + odd) % 8, (z + odd) % 8
    step = (at % 2) ^ (me % 2)
    turns = (at // 2 - me // 2 + 4) % 4
    across = (owner // 2 % 2) ^ pair
    place = jnp.where(late == 1, (across * 2 + odd) * 2 + step, (step * 2 + odd) * 2 + across)
    place = ((1 - late) * 8 + place) * 8 + turns * 2 + within % 2
    block = (tile_rows - (z * 4 + pair * 2 + core) * 16) ^ (half * 8)
    which = jnp.where((owner % 2) ^ core == 1, 1 - late, 2)
    place = place - jnp.where(which == 1, PLACES, 0)
    table = list_table(tile_live, block * 256 + place, which)

    table, _ = lax.optimization_barrier((table, near))
    part, table = lax.optimization_barrier((part, table))
    lists, starts, tiles = make_lists(table, tile_vals)
    far = lax.ppermute(near, "half", swap(2))
    part, far = beside(steps, 1, part, far)
    self_term = both[rows:]


    (away,) = tile_sums(0, 1, lists, starts, near, far, tiles, jnp.bfloat16)
    came_late = lax.ppermute(away, "core", swap(2))
    near, _ = lax.optimization_barrier((near, away))
    (away,) = tile_sums(1, 1, lists, starts, near, far, tiles, jnp.bfloat16)
    came_early = lax.ppermute(away, "core", swap(2))
    late, early = tile_sums(2, 2, lists, starts, near, far, tiles, jnp.float32)
    late = under(late + wide(came_late), (2, 2, 2, 4, 2))
    came_late = lax.ppermute(half16(late[1]), "pair", swap(2))
    early = under(early + wide(came_early), (2, 2, 2, 4, 2))
    even, odd_ones = half16(early[1, 0]), half16(early[1, 1])
    part, even, odd_ones = lax.optimization_barrier((part, even, odd_ones))
    came_even = lax.ppermute(even, "z", EVEN_PAIRS)
    came_odd = lax.ppermute(odd_ones, "z", ODD_PAIRS)
    part, came_even, came_odd, came_late = beside(steps, 1, part, came_even, came_odd, came_late)

    early = early[0] + wide(jnp.stack([came_even, came_odd]))
    late = late[0] + wide(came_late)
    across, even, odd_ones = half16(early[:, 1]), half16(late[0, 1]), half16(late[1, 1])
    part, across, even, odd_ones = lax.optimization_barrier((part, across, even, odd_ones))
    came_early = lax.ppermute(across, "pair", swap(2))
    came_even = lax.ppermute(even, "z", EVEN_PAIRS)
    came_odd = lax.ppermute(odd_ones, "z", ODD_PAIRS)
    part, came_early, came_even, came_odd = beside(steps, 1, part, came_early, came_even, came_odd)

    early = early[:, 0] + wide(came_early)
    late = late[:, 0] + wide(jnp.stack([came_even, came_odd]))
    both = jnp.concatenate([early, late], axis=0)
    rounded = half16(both)
    part, rounded = lax.optimization_barrier((part, rounded))
    came = [lax.ppermute(rounded[:, k], "z", turn(2 * k, 8)) for k in (3, 1, 2)]
    part = next(steps)(next(steps)(part))
    other = lax.ppermute(part, "core", swap(2))
    grads = jnp.where(core == 0, part, other), jnp.where(core == 0, other, part)
    summed = both[:, 0] + wide(came[0]) + wide(came[1]) + wide(came[2])
    summed = summed.reshape(8, rows, BLOCK).transpose(1, 0, 2).reshape(rows, nodes)
    input_grad = half16(summed + self_term)
    return (input_grad, *grads)


def solution(mesh):
    nodes = ("z", "pair", "core", "half")
    return jax.shard_map(
        on_device,
        mesh=Mesh(mesh.devices.reshape(8, 2, 2, 2, 4), AXES),
        in_specs=(
            P("x", nodes),
            P("x", nodes),
            P(None, nodes),
            P(None, nodes),
            P(),
            P(),
            P(nodes),
            P(nodes),
            P(nodes, None, None),
            P(nodes),
        ),
        out_specs=(P("x", nodes), P(None, "x"), P(None, "x")),
        check_vma=False,
    )
```

```python
import jax
import jax.numpy as jnp
from jax import lax
from jax.experimental import pallas as pl
from jax.experimental.pallas import tpu as pltpu
from jax.sharding import Mesh, PartitionSpec as P

AXES = ("z", "pair", "core", "half", "x")
BLOCK = 128
GROUP = 16
BIG = 64
CHUNK = 32
LISTS = 3
PLACES = 64
ROOM = 256 + LISTS * GROUP
SCOPED = 16 * 1024 * 1024


def swap(n):
    return [(i, i ^ 1) for i in range(n)]


def turn(k, n):
    return [(i, (i + k) % n) for i in range(n)]


EVEN_PAIRS = swap(8)
ODD_PAIRS = [(i, (((i + 1) % 8 ^ 1) - 1) % 8) for i in range(8)]


def list_kernel(table_ref, vals_ref, lists_ref, starts_ref, tiles_ref, sem):
    slots = vals_ref.shape[0]
    live = table_ref[2 * slots + 8]
    chunks = (live + CHUNK - 1) // CHUNK

    def fetch(chunk, carry):
        some = pl.ds(chunk * CHUNK, CHUNK)
        pltpu.make_async_copy(vals_ref.at[some], tiles_ref.at[some], sem).start()
        return carry

    lax.fori_loop(0, chunks, fetch, 0)
    starts_ref[0] = table_ref[2 * slots]
    for i in range(1, LISTS + 1):
        end = table_ref[2 * slots + i]
        starts_ref[i] = end
        for k in range(GROUP - 1):
            lists_ref[jnp.maximum(end - 1 - k, 0)] = jnp.int32(2 * PLACES)

    def place(step, carry):
        for k in range(GROUP):
            slot = step * GROUP + k
            lists_ref[table_ref[slot]] = table_ref[slots + slot]
        return carry

    def finish(chunk, carry):
        some = pl.ds(0, CHUNK)
        pltpu.make_async_copy(vals_ref.at[some], tiles_ref.at[some], sem).wait()
        return carry

    lax.fori_loop(0, (live + GROUP - 1) // GROUP, place, 0)
    lax.fori_loop(0, chunks, finish, 0)


def list_table(live, entries, which):
    slots = jnp.arange(entries.shape[0], dtype=jnp.int32)
    which = jnp.where(slots < live, which, LISTS)
    earlier = (which[:, None] == which[None, :]) & (slots[:, None] > slots[None, :])
    rank = jnp.sum(earlier.astype(jnp.int32), axis=1)
    lists = jnp.arange(8, dtype=jnp.int32)
    member = which[:, None] == lists[None, :]
    held = jnp.sum(member.astype(jnp.int32), axis=0)
    room = (held + GROUP - 1) // GROUP * GROUP
    starts = jnp.sum(jnp.where(lists[:, None] < lists[None, :], room[:, None], 0), axis=0)
    first = jnp.sum(jnp.where(member, starts[None, :], 0), axis=1)
    spots = jnp.where(which < LISTS, first + rank, ROOM + slots % GROUP)
    return jnp.concatenate([spots, slots * 65536 + entries, starts, live])


def make_lists(table, vals):
    smem = pl.BlockSpec(memory_space=pltpu.SMEM)
    return pl.pallas_call(
        list_kernel,
        out_shape=(
            pltpu.SMEM((ROOM + GROUP,), jnp.int32),
            pltpu.SMEM((LISTS + 1,), jnp.int32),
            pltpu.VMEM(vals.shape, vals.dtype),
        ),
        in_specs=[smem, pl.BlockSpec(memory_space=pl.ANY)],
        out_specs=(smem, smem, pl.BlockSpec(memory_space=pltpu.VMEM)),
        scratch_shapes=[pltpu.SemaphoreType.DMA],
        compiler_params=pltpu.CompilerParams(vmem_limit_bytes=SCOPED),
        cost_estimate=pl.CostEstimate(flops=0, bytes_accessed=12 << 20, transcendentals=0),
    )(table, pltpu.with_memory_space_constraint(vals, pltpu.HBM))


def tile_kernel(which, lists_ref, starts_ref, near_ref, far_ref, tiles_ref, *refs):
    *outs, total, panel = refs
    start, end = starts_ref[which], starts_ref[which + 1]
    panel[0:8] = near_ref[...]
    panel[8:16] = far_ref[...]
    used = len(outs) * PLACES
    total[0:used] = jnp.zeros((used, *total.shape[1:]), total.dtype)

    def add(base, count):
        entries = [lists_ref[base + k] for k in range(count)]
        products = [
            jnp.dot(panel[entry // 256 & 255], tiles_ref[entry // 65536], preferred_element_type=jnp.float32)
            for entry in entries
        ]
        for entry, product in zip(entries, products):
            total[entry & 255] += product

    def big(step, carry):
        add(start + step * BIG, BIG)
        return carry

    count = end - start
    lax.fori_loop(0, count // BIG, big, 0)
    size = BIG // 2
    while size >= GROUP:
        pl.when(count & size != 0)(lambda size=size: add(start + count // (2 * size) * (2 * size), size))
        size //= 2
    for i, out_ref in enumerate(outs):
        out_ref[...] = total[i * PLACES : (i + 1) * PLACES].astype(out_ref.dtype)


def tile_sums(which, outs, lists, starts, near, far, tiles, dtype):
    rows = near.shape[1]
    smem = pl.BlockSpec(memory_space=pltpu.SMEM)
    vmem = pl.BlockSpec(memory_space=pltpu.VMEM)
    return pl.pallas_call(
        lambda *refs: tile_kernel(which, *refs),
        out_shape=(jax.ShapeDtypeStruct((PLACES, rows, BLOCK), dtype),) * outs,
        in_specs=[smem, smem, vmem, vmem, vmem],
        out_specs=(vmem,) * outs,
        scratch_shapes=[
            pltpu.VMEM((2 * PLACES + 1, rows, BLOCK), jnp.float32),
            pltpu.VMEM((16, rows, BLOCK), jnp.bfloat16),
        ],
        compiler_params=pltpu.CompilerParams(vmem_limit_bytes=SCOPED),
        cost_estimate=pl.CostEstimate(flops=2 * 64 * rows * 128 * 128, bytes_accessed=4 << 20, transcendentals=0),
    )(
        pltpu.with_memory_space_constraint(lists, pltpu.SMEM),
        pltpu.with_memory_space_constraint(starts, pltpu.SMEM),
        near,
        far,
        pltpu.with_memory_space_constraint(tiles, pltpu.VMEM),
    )


def half16(x):
    return x.astype(jnp.bfloat16)


def wide(x):
    return x.astype(jnp.float32)


def under(core_sum, shape):
    return core_sum.reshape(*shape, *core_sum.shape[1:])


def weight_steps():
    def give(axis):
        me = lax.axis_index(axis)

        def step(part):
            n = part.shape[0] // 2
            mine = lax.dynamic_slice_in_dim(part, me * n, n, 0)
            other = lax.dynamic_slice_in_dim(part, (1 - me) * n, n, 0)
            return mine + lax.ppermute(other, axis, swap(2))

        return step

    def join(axis, k):
        return lambda part: part + lax.ppermute(part, axis, [(i, i ^ k) for i in range(lax.axis_size(axis))])

    return iter(
        [give("core"), join("z", 1), join("z", 4), join("z", 2), join("half", 1), join("pair", 1)]
    )


def beside(steps, count, part, *others):
    for _ in range(count):
        part = next(steps)(part)
    return lax.optimization_barrier((part, *others))


def contract_nodes(left, right):
    return lax.dot_general(left, right, (((1,), (1,)), ((), ())), preferred_element_type=jnp.float32)


def on_device(
    cotangent, preact, features, aggregated, w_self, w_neigh, tile_rows, tile_cols, tile_vals, tile_live
):
    z, pair, core, half, x = (lax.axis_index(a) for a in AXES)
    delta = jnp.where(preact > 0, cotangent, jnp.zeros_like(cotangent))
    rows, nodes = delta.shape

    steps = weight_steps()
    part = jnp.concatenate([contract_nodes(features, delta), contract_nodes(aggregated, delta)], axis=0)
    hidden = [lax.ppermute(delta, "x", turn(k, 4)) for k in (3, 2, 1)]
    part, *hidden = beside(steps, 1, part, *hidden)
    hidden = [delta] + hidden
    weights = jnp.concatenate(
        [lax.dynamic_slice_in_dim(w, x * rows, rows, 0) for w in (w_neigh, w_self)], axis=0
    )
    weights = jnp.concatenate(
        [lax.dynamic_slice_in_dim(weights, (x + 4 - k) % 4 * rows, rows, 1) for k in (0, 3, 2, 1)], axis=1
    )
    both = jnp.dot(weights, jnp.concatenate(hidden, axis=0), preferred_element_type=jnp.float32)
    near = half16(both[:rows]).reshape(rows, nodes // BLOCK, BLOCK).transpose(1, 0, 2)
    owner, within = tile_cols // 16, tile_cols % 8
    late, odd = within // 4, within // 2 % 2
    at, me = (owner // 4 + odd) % 8, (z + odd) % 8
    step = (at % 2) ^ (me % 2)
    turns = (at // 2 - me // 2 + 4) % 4
    across = (owner // 2 % 2) ^ pair
    place = jnp.where(late == 1, (across * 2 + odd) * 2 + step, (step * 2 + odd) * 2 + across)
    place = ((1 - late) * 8 + place) * 8 + turns * 2 + within % 2
    block = (tile_rows - (z * 4 + pair * 2 + core) * 16) ^ (half * 8)
    which = jnp.where((owner % 2) ^ core == 1, 1 - late, 2)
    place = place - jnp.where(which == 1, PLACES, 0)
    table = list_table(tile_live, block * 256 + place, which)

    table, _ = lax.optimization_barrier((table, near))
    part, table = lax.optimization_barrier((part, table))
    lists, starts, tiles = make_lists(table, tile_vals)
    far = lax.ppermute(near, "half", swap(2))
    part, far = beside(steps, 1, part, far)
    self_term = both[rows:]


    (away,) = tile_sums(0, 1, lists, starts, near, far, tiles, jnp.bfloat16)
    came_late = lax.ppermute(away, "core", swap(2))
    near, _ = lax.optimization_barrier((near, away))
    (away,) = tile_sums(1, 1, lists, starts, near, far, tiles, jnp.bfloat16)
    came_early = lax.ppermute(away, "core", swap(2))
    late, early = tile_sums(2, 2, lists, starts, near, far, tiles, jnp.float32)
    late = under(late + wide(came_late), (2, 2, 2, 4, 2))
    came_late = lax.ppermute(half16(late[1]), "pair", swap(2))
    early = under(early + wide(came_early), (2, 2, 2, 4, 2))
    even, odd_ones = half16(early[1, 0]), half16(early[1, 1])
    part, even, odd_ones = lax.optimization_barrier((part, even, odd_ones))
    came_even = lax.ppermute(even, "z", EVEN_PAIRS)
    came_odd = lax.ppermute(odd_ones, "z", ODD_PAIRS)
    part, came_even, came_odd, came_late = beside(steps, 1, part, came_even, came_odd, came_late)

    early = early[0] + wide(jnp.stack([came_even, came_odd]))
    late = late[0] + wide(came_late)
    across, even, odd_ones = half16(early[:, 1]), half16(late[0, 1]), half16(late[1, 1])
    part, across, even, odd_ones = lax.optimization_barrier((part, across, even, odd_ones))
    came_early = lax.ppermute(across, "pair", swap(2))
    came_even = lax.ppermute(even, "z", EVEN_PAIRS)
    came_odd = lax.ppermute(odd_ones, "z", ODD_PAIRS)
    part, came_early, came_even, came_odd = beside(steps, 1, part, came_early, came_even, came_odd)

    early = early[:, 0] + wide(came_early)
    late = late[:, 0] + wide(jnp.stack([came_even, came_odd]))
    both = jnp.concatenate([early, late], axis=0)
    rounded = half16(both)
    part, rounded = lax.optimization_barrier((part, rounded))
    came = [lax.ppermute(rounded[:, k], "z", turn(2 * k, 8)) for k in (3, 1, 2)]
    part = next(steps)(next(steps)(part))
    other = lax.ppermute(part, "core", swap(2))
    grads = jnp.where(core == 0, part, other), jnp.where(core == 0, other, part)
    summed = both[:, 0] + wide(came[0]) + wide(came[1]) + wide(came[2])
    summed = summed.reshape(8, rows, BLOCK).transpose(1, 0, 2).reshape(rows, nodes)
    input_grad = half16(summed + self_term)
    return (input_grad, *grads)


def solution(mesh):
    nodes = ("z", "pair", "core", "half")
    return jax.shard_map(
        on_device,
        mesh=Mesh(mesh.devices.reshape(8, 2, 2, 2, 4), AXES),
        in_specs=(
            P("x", nodes),
            P("x", nodes),
            P(None, nodes),
            P(None, nodes),
            P(),
            P(),
            P(nodes),
            P(nodes),
            P(nodes, None, None),
            P(nodes),
        ),
        out_specs=(P("x", nodes), P(None, "x"), P(None, "x")),
        check_vma=False,
    )
```
